256 devices in a mesh: seq: 64 (over y, z, x_hi), head: 4 (over x_lo, core).
Axes of the slice: x: 4 (x_hi: 2, x_lo: 2; x = x_hi * 2 + x_lo), y: 4, z: 8, core: 2. Of those that a mesh axis runs over, the one named last changes fastest.
Arguments:
- text_rows: bfloat16 [32768, 8192], P('seq', 'head'), may hold values from -12 to 12
- text_gain: bfloat16 [8192], P('head'), may hold values from 0.5 to 4
- query_weight: bfloat16 [8192, 4096], P('seq', 'head'), may hold values from -0.0625 to 0.0625
- key_weight: bfloat16 [1280, 4096], P('seq', 'head'), may hold values from -0.15625 to 0.15625
- value_weight: bfloat16 [1280, 4096], P('seq', 'head'), may hold values from -0.15625 to 0.15625
- images: bfloat16 [128, 256, 1280], P('seq'), may hold values from -6 to 6
- patch_counts: int32 [128], P('seq'), may hold values from 64 to 256, as said below
- image_counts: int32 [64], P('seq'), may hold values from 0 to 2, as said below
- image_spans: int32 [2, 128], P(None, 'seq'), may hold values from 0 to 32768, as said below
- latents: bfloat16 [64, 1280], replicated, may hold values from -6 to 6
- latent_gain: bfloat16 [1280], replicated, may hold values from 0.5 to 4
- context_gain: bfloat16 [1280], replicated, may hold values from 0.5 to 4
- final_gain: bfloat16 [1280], replicated, may hold values from 0.5 to 4
- res_query: bfloat16 [1280, 1536], P(None, 'head'), may hold values from -0.15625 to 0.15625
- res_key: bfloat16 [1280, 1536], P(None, 'head'), may hold values from -0.15625 to 0.15625
- res_value: bfloat16 [1280, 1536], P(None, 'head'), may hold values from -0.15625 to 0.15625
- res_output: bfloat16 [1536, 1280], P('head'), may hold values from -0.15625 to 0.15625
Outputs:
- attended: bfloat16 [32768, 4096], P('seq', 'head')
The draws below stay inside these ranges and needn't reach their ends.
Inputs may be any that keep to these rules, and one draw needn't show every extreme that they name: `image_spans`: row 0 holds span starts, row 1 span ends. For live slots (see image_counts) a span starts inside its owner shard's 512 tokens, is nonempty, ends no later than 1024 tokens after its start, and live spans are disjoint; some span reaches tokens of the shard 2 after its owner. Bounds of slots that are not live carry no meaning. `image_counts`: images owned by each seq shard, its live slots being the first ones; some shard owns 2. `patch_counts`: patches past the count are padding; every shard has a slot with 256 and a slot with 64 live patches.
All inputs are finite; a program needn't handle non-finite values.
Results may differ from the reference program's by a relative error of at most 0.024.
The reference program's roundings to bfloat16 on the way count: a program that leaves them out, or rounds other values in their place, can miss the bound.
Values may be sent and summed in bfloat16 or wider, within the bound.
No kernel may reach another device: no remote copies, remote signals or barrier semaphores. Data moves between devices by JAX's collectives and lax.ppermute only.
A program may use at most 128 MiB of HBM per device.

```python
import math
import jax
import jax.numpy as jnp
from jax import lax

D = 8192
HEADS = 32
HD = 128
VW = 1280
RHEADS = 16
RHD = 96
LAT = 64
PATCH = 256
REACH = 2
IMG_CAP = 2
TOK_DEV = 512
TOKENS = 32768
IMAGES = 128
N_SEQ = 64


def span_layout(key):
    shards = TOKENS // TOK_DEV
    slots = shards * IMG_CAP
    key_busy, key_coin, key_many, key_few, key_place = jax.random.split(key, 5)
    busiest = jax.random.randint(key_busy, (), 0, shards - REACH)
    coin_flips = jax.random.randint(key_coin, (shards,), 0, 2)
    many_images = jax.random.randint(key_many, (shards,), 1, IMG_CAP + 1)
    few_images = jax.random.randint(key_few, (shards,), 0, 2)
    counts = jnp.where(coin_flips == 1, many_images, few_images)
    shard_ids = jnp.arange(shards)
    counts = jnp.where(shard_ids == busiest, IMG_CAP, counts)
    counts = jnp.where((shard_ids > busiest) & (shard_ids <= busiest + REACH), 0, counts)
    ranking = jax.random.randint(key_place, (shards, TOK_DEV - 1), 0, 1 << 16) * (TOK_DEV - 1) + jnp.arange(TOK_DEV - 1)[None, :]
    offsets = jnp.sort(jnp.argsort(ranking, axis=1, stable=True)[:, :IMG_CAP] + 1, axis=1)
    starts = (shard_ids[:, None] * TOK_DEV + offsets).reshape(slots)
    live_slot = (jnp.arange(IMG_CAP)[None, :] < counts[:, None]).reshape(slots)
    later = live_slot[None, :] & (starts[None, :] > starts[:, None])
    following = jnp.min(jnp.where(later, starts[None, :], TOKENS), axis=1)
    ends = jnp.minimum(jnp.minimum(following, starts + REACH * TOK_DEV), TOKENS)
    owner_base = jnp.repeat(shard_ids * TOK_DEV, IMG_CAP)
    starts = jnp.where(live_slot, starts, owner_base)
    ends = jnp.where(live_slot, ends, owner_base + TOK_DEV)
    return (counts.astype(jnp.int32), jnp.stack([starts, ends]).astype(jnp.int32))


def draw_image_counts(key, part):
    counts, bounds = span_layout(key)
    return counts


def draw_image_spans(key, part):
    counts, bounds = span_layout(key)
    return bounds


def draw_patch_counts(key, part):
    key = jax.random.fold_in(key, 5)
    shards = TOKENS // TOK_DEV
    key_live, key_slot = jax.random.split(key)
    live = jax.random.randint(key_live, (shards, IMG_CAP), PATCH // 4, PATCH + 1)
    full_slot = jax.random.randint(key_slot, (shards, 1), 0, IMG_CAP)
    column = jnp.arange(IMG_CAP)[None, :]
    live = jnp.where(column == full_slot, PATCH, live)
    live = jnp.where(column == (full_slot + 1) % IMG_CAP, PATCH // 4, live)
    return live.reshape(shards * IMG_CAP).astype(jnp.int32)


def rising_rows(key, top):
    key_rough, key_body = jax.random.split(key)
    column = jnp.arange(D, dtype=jnp.float32) / (D - 1)
    rough = jax.random.uniform(key_rough, (D,), jnp.float32, 0.7, 1.3)
    column_scale = jnp.exp(column * math.log(top)) * rough
    entries = jax.random.normal(key_body, (TOKENS, D), jnp.float32)
    return jnp.clip(entries * column_scale[None, :], -12.0, 12.0).astype(jnp.bfloat16)


def draw_text_rows(key, part):
    key = jax.random.fold_in(key, 23)
    return rising_rows(key, 2.5)


def gain_values(key, count, lowest, highest):
    return jnp.exp(jax.random.uniform(key, (count,), jnp.float32, math.log(lowest), math.log(highest))).astype(jnp.bfloat16)


def draw_text_gain(key, part):
    key = jax.random.fold_in(key, 11)
    return gain_values(key, D, 0.5, 2.0)


def draw_latent_gain(key, part):
    key = jax.random.fold_in(key, 13)
    return gain_values(key, VW, 0.5, 2.0)


def draw_context_gain(key, part):
    key = jax.random.fold_in(key, 17)
    return gain_values(key, VW, 0.5, 2.0)


def draw_final_gain(key, part):
    key = jax.random.fold_in(key, 19)
    return gain_values(key, VW, 0.5, 2.0)


def steps_of(key, shape, cuts, least, largest):
    loudness = 1.0
    for dim, parts in cuts:
        draws = jax.random.uniform(jax.random.fold_in(jax.random.fold_in(key, 6), dim), (parts,), jnp.float32, least / len(cuts), largest / len(cuts))
        loudness = loudness * jnp.repeat(jnp.exp(draws), shape[dim] // parts).reshape((-1,) + (1,) * (len(shape) - 1 - dim))
    return loudness


def scatter_about(stream_key, dims, deviation, limit, cuts=(), kind=jnp.bfloat16):
    drawn = deviation * jax.random.normal(stream_key, dims, jnp.float32)
    if cuts:
        drawn = drawn * steps_of(stream_key, dims, cuts, -0.22, 0.18)
    return jnp.clip(drawn, -limit, limit).astype(kind)


def setup_inputs(seed: int = 0) -> dict:
    splits = jax.random.split(jax.random.key(seed), 18)
    return {
        "text_rows": draw_text_rows(jax.random.fold_in(splits[17], 71), 0),
        "text_gain": draw_text_gain(jax.random.fold_in(splits[17], 71), 0),
        "query_weight": scatter_about(splits[2], (D, HEADS * HD), D ** -0.5, 0.0625, ((0, 64), (1, 4))),
        "key_weight": scatter_about(splits[3], (VW, HEADS * HD), VW ** -0.5, 0.15625, ((0, 64), (1, 4))),
        "value_weight": scatter_about(splits[4], (VW, HEADS * HD), VW ** -0.5, 0.15625, ((0, 64), (1, 4))),
        "images": scatter_about(splits[5], (IMAGES, PATCH, VW), 1.0, 6.0, ((0, 64),)),
        "patch_counts": draw_patch_counts(jax.random.fold_in(splits[17], 71), 0),
        "image_counts": draw_image_counts(jax.random.fold_in(splits[17], 71), 0),
        "image_spans": draw_image_spans(jax.random.fold_in(splits[17], 71), 0),
        "latents": scatter_about(splits[9], (LAT, VW), 1.0, 6.0),
        "latent_gain": draw_latent_gain(jax.random.fold_in(splits[17], 71), 0),
        "context_gain": draw_context_gain(jax.random.fold_in(splits[17], 71), 0),
        "final_gain": draw_final_gain(jax.random.fold_in(splits[17], 71), 0),
        "res_query": scatter_about(splits[13], (VW, RHEADS * RHD), VW ** -0.5, 0.15625, ((1, 4),)),
        "res_key": scatter_about(splits[14], (VW, RHEADS * RHD), VW ** -0.5, 0.15625, ((1, 4),)),
        "res_value": scatter_about(splits[15], (VW, RHEADS * RHD), VW ** -0.5, 0.15625, ((1, 4),)),
        "res_output": scatter_about(splits[16], (RHEADS * RHD, VW), (RHEADS * RHD) ** -0.5, 0.15625, ((0, 4),)),
    }


EPS_TEXT = 1e-06
EPS_VISION = 1e-05
FILL = -1e+30

def layer_norm(values, gain):
    middle = lax.optimization_barrier(jnp.mean(values, axis=-1, keepdims=True))
    centred = values - middle
    spread = lax.optimization_barrier(jnp.mean(centred * centred, axis=-1, keepdims=True))
    return centred * lax.rsqrt(spread + EPS_VISION) * gain

def masked_softmax(scores, allowed):
    highest = lax.optimization_barrier(jnp.max(jnp.where(allowed, scores, FILL), axis=-1, keepdims=True))
    weights = jnp.where(allowed, jnp.exp(scores - highest), 0.0)
    summed = lax.optimization_barrier(jnp.sum(weights, axis=-1, keepdims=True))
    anything = jnp.any(allowed, axis=-1, keepdims=True)
    return (weights / jnp.where(anything, summed, 1.0)).astype(jnp.bfloat16)

def reference(text_rows, text_gain, query_weight, key_weight, value_weight, images, patch_counts, image_counts, image_spans, latents, latent_gain, context_gain, final_gain, res_query, res_key, res_value, res_output):
    source = text_rows.astype(jnp.float32)
    power = lax.optimization_barrier(jnp.mean(source * source, axis=-1, keepdims=True))
    normed_text = (source * lax.rsqrt(power + EPS_TEXT) * text_gain.astype(jnp.float32)).astype(jnp.bfloat16)
    queries = jnp.dot(normed_text, query_weight, preferred_element_type=jnp.float32).astype(jnp.bfloat16)
    latent_base = latents.astype(jnp.float32)
    latent_normed = layer_norm(latent_base, latent_gain.astype(jnp.float32)).astype(jnp.bfloat16)
    latent_queries = jnp.dot(latent_normed, res_query, preferred_element_type=jnp.float32).astype(jnp.bfloat16).reshape(LAT, RHEADS, RHD)
    key_rows = jnp.arange(PATCH + LAT, dtype=jnp.int32)

    def resample_one(item):
        image, live = item
        context_normed = layer_norm(image.astype(jnp.float32), context_gain.astype(jnp.float32)).astype(jnp.bfloat16)
        joined = jnp.concatenate([context_normed, latent_normed], axis=0)
        res_keys = jnp.dot(joined, res_key, preferred_element_type=jnp.float32).astype(jnp.bfloat16).reshape(PATCH + LAT, RHEADS, RHD)
        res_values = jnp.dot(joined, res_value, preferred_element_type=jnp.float32).astype(jnp.bfloat16).reshape(PATCH + LAT, RHEADS, RHD)
        scores = jnp.einsum('qhd,khd->hqk', latent_queries.astype(jnp.float32), res_keys.astype(jnp.float32)) * RHD ** (-0.5)
        allowed = (key_rows < live) | (key_rows >= PATCH)
        res_probs = masked_softmax(scores, allowed[None, None, :])
        res_heads = jnp.einsum('hqk,khd->qhd', res_probs.astype(jnp.float32), res_values.astype(jnp.float32)).astype(jnp.bfloat16).reshape(LAT, RHEADS * RHD)
        mixed = jnp.dot(res_heads, res_output, preferred_element_type=jnp.float32)
        return layer_norm(latent_base + mixed, final_gain.astype(jnp.float32)).astype(jnp.bfloat16)
    resampled = lax.map(resample_one, (images, patch_counts))
    flat_latents = resampled.reshape(IMAGES * LAT, VW)
    cross_keys = jnp.dot(flat_latents, key_weight, preferred_element_type=jnp.float32).astype(jnp.bfloat16).reshape(IMAGES, LAT, HEADS * HD)
    cross_values = jnp.dot(flat_latents, value_weight, preferred_element_type=jnp.float32).astype(jnp.bfloat16).reshape(IMAGES, LAT, HEADS * HD)
    live_slot = (jnp.arange(IMG_CAP, dtype=jnp.int32)[None, :] < image_counts[:, None]).reshape(IMAGES)
    starts = jnp.where(live_slot, image_spans[0], 0).astype(jnp.int32)
    ends = jnp.where(live_slot, image_spans[1], 0).astype(jnp.int32)
    padding = REACH * IMG_CAP
    keys_padded = jnp.concatenate([jnp.zeros((padding, LAT, HEADS * HD), jnp.bfloat16), cross_keys], axis=0)
    values_padded = jnp.concatenate([jnp.zeros((padding, LAT, HEADS * HD), jnp.bfloat16), cross_values], axis=0)
    starts_padded = jnp.concatenate([jnp.zeros((padding,), jnp.int32), starts], axis=0)
    ends_padded = jnp.concatenate([jnp.zeros((padding,), jnp.int32), ends], axis=0)
    window = (REACH + 1) * IMG_CAP
    blocks = queries.reshape(N_SEQ, TOK_DEV, HEADS, HD)

    def attend(item):
        shard, block = item
        first = (shard * IMG_CAP).astype(jnp.int32)
        near_keys = lax.dynamic_slice_in_dim(keys_padded, first, window, 0).reshape(window * LAT, HEADS, HD)
        near_values = lax.dynamic_slice_in_dim(values_padded, first, window, 0).reshape(window * LAT, HEADS, HD)
        near_starts = lax.dynamic_slice_in_dim(starts_padded, first, window, 0)
        near_ends = lax.dynamic_slice_in_dim(ends_padded, first, window, 0)
        position = shard * TOK_DEV + jnp.arange(TOK_DEV, dtype=jnp.int32)
        seen = (position[:, None] >= near_starts[None, :]) & (position[:, None] < near_ends[None, :])
        seen = jnp.broadcast_to(seen[:, :, None], (TOK_DEV, window, LAT)).reshape(TOK_DEV, window * LAT)
        scores = jnp.einsum('thd,khd->htk', block.astype(jnp.float32), near_keys.astype(jnp.float32)) * HD ** (-0.5)
        cross_probs = masked_softmax(scores, seen[None])
        context = jnp.einsum('htk,khd->thd', cross_probs.astype(jnp.float32), near_values.astype(jnp.float32)).astype(jnp.bfloat16)
        return context.reshape(TOK_DEV, HEADS * HD)
    attended = lax.map(attend, (jnp.arange(N_SEQ, dtype=jnp.int32), blocks))
    return attended.reshape(TOKENS, HEADS * HD)
```

```python
import functools

import jax
import jax.numpy as jnp
from jax import lax
from jax.experimental import pallas as pl
from jax.experimental.pallas import tpu as pltpu
from jax.sharding import Mesh, PartitionSpec as P

D = 8192
HD = 128
RHD = 96
LAT = 64
PATCH = 256
VW = 1280

EPS_TEXT = 1e-06
EPS_VISION = 1e-05
FILL = -1e30

NY, NZ, NX = 4, 8, 4
TOK = 512
COLS = 512
KEYS = 512
ROWS = 128


def layer_norm(values, gain):
    middle = jnp.mean(values, axis=-1, keepdims=True)
    centred = values - middle
    spread = jnp.mean(centred * centred, axis=-1, keepdims=True)
    return centred * lax.rsqrt(spread + EPS_VISION) * gain


def masked_softmax(scores, allowed):
    highest = jnp.max(jnp.where(allowed, scores, FILL), axis=-1, keepdims=True)
    weights = jnp.where(allowed, jnp.exp(scores - highest), 0.0)
    summed = jnp.sum(weights, axis=-1, keepdims=True)
    anything = jnp.any(allowed, axis=-1, keepdims=True)
    return (weights / jnp.where(anything, summed, 1.0)).astype(jnp.bfloat16)


def turned(x, axis, by, count):
    return lax.ppermute(x, axis, [(i, (i + by) % count) for i in range(count)])


def next_pair(x):
    return lax.ppermute(x, ("y", "z"), [(i, i + 1) for i in range(NY * NZ - 1)])


def absolute(blocks, axis, place, count):
    twice = jnp.concatenate([blocks, blocks], axis=axis)
    return lax.dynamic_slice_in_dim(twice, (count - place) % count, count, axis)


def relative(blocks, axis, place, count):
    twice = jnp.concatenate([blocks, blocks], axis=axis)
    return lax.dynamic_slice_in_dim(twice, place, count, axis)


def gather_rows(early, late):
    e1 = turned(early, "y", -1, NY)
    e3 = turned(early, "y", 1, NY)
    e2 = turned(early, "y", 2, NY)
    plus = [late]
    minus = [late]
    plus.append(turned(plus[-1], "z", -1, NZ))
    minus.append(turned(minus[-1], "z", 1, NZ))
    column = jnp.stack([early, e1, e2, e3])
    for _ in range(2):
        plus.append(turned(plus[-1], "z", -1, NZ))
        minus.append(turned(minus[-1], "z", 1, NZ))
    cut = late.shape[0] // 2
    far = jnp.concatenate(
        [turned(plus[3][:cut], "z", -1, NZ), turned(minus[3][cut:], "z", 1, NZ)], axis=0
    )
    row = jnp.stack([plus[0], plus[1], plus[2], plus[3], far, minus[3], minus[2], minus[1]])
    cplus = [column]
    cminus = [column]
    for _ in range(3):
        cplus.append(turned(cplus[-1], "z", -1, NZ))
        cminus.append(turned(cminus[-1], "z", 1, NZ))
    cfar = jnp.concatenate(
        [turned(cplus[3][:2], "z", -1, NZ), turned(cminus[3][2:], "z", 1, NZ)], axis=0
    )
    r1 = turned(row, "y", -1, NY)
    r3 = turned(row, "y", 1, NY)
    r2 = turned(row, "y", 2, NY)
    early_all = jnp.stack(
        [cplus[0], cplus[1], cplus[2], cplus[3], cfar, cminus[3], cminus[2], cminus[1]], axis=1
    )
    late_all = jnp.stack([row, r1, r2, r3])
    return early_all, late_all


def attend_kernel(where_ref, text_ref, weight_ref, scale_ref, key_ref, value_ref, bound_ref, out_ref, acc_ref):
    step = pl.program_id(0)
    part = jnp.dot(text_ref[0], weight_ref[...], preferred_element_type=jnp.float32)

    @pl.when(step == 0)
    def _():
        acc_ref[...] = part

    @pl.when(step > 0)
    def _():
        acc_ref[...] += part

    @pl.when(step == NY - 1)
    def _():
        position = where_ref[1] + lax.broadcasted_iota(jnp.int32, (TOK, KEYS), 0)
        seen = (position >= bound_ref[0:1, :]) & (position < bound_ref[1:2, :])
        anything = jnp.any(seen, axis=-1, keepdims=True)
        for head in range(COLS // HD):
            cols = pl.ds(head * HD, HD)
            queries = (acc_ref[:, cols] * scale_ref[...]).astype(jnp.bfloat16)
            scores = lax.dot_general(
                queries, key_ref[:, cols], (((1,), (1,)), ((), ())), preferred_element_type=jnp.float32
            ) * HD ** (-0.5)
            scores = jnp.where(seen, scores, FILL)
            highest = jnp.max(scores, axis=-1, keepdims=True)
            weights = jnp.where(seen, jnp.exp(scores - highest), 0.0)
            summed = jnp.sum(weights, axis=-1, keepdims=True)
            probs = (weights * (1.0 / jnp.where(anything, summed, 1.0))).astype(jnp.bfloat16)
            out_ref[:, cols] = jnp.dot(
                probs, value_ref[:, cols], preferred_element_type=jnp.float32
            ).astype(jnp.bfloat16)


def attend(half, pair, text, weight, scale, keys, values, bounds):
    where = jnp.stack([half, pair * (2 * TOK) + half * TOK]).astype(jnp.int32)
    return pl.pallas_call(
        attend_kernel,
        out_shape=jax.ShapeDtypeStruct((TOK, COLS), jnp.bfloat16),
        grid_spec=pltpu.PrefetchScalarGridSpec(
            num_scalar_prefetch=1,
            grid=(NY,),
            in_specs=[
                pl.BlockSpec((1, TOK, D // NY), lambda k, w: (w[0] * NY + k, 0, 0)),
                pl.BlockSpec((D // NY, COLS), lambda k, w: (k, 0)),
                pl.BlockSpec((TOK, 1), lambda k, w: (w[0], 0)),
                pl.BlockSpec((KEYS, COLS), lambda k, w: (0, 0)),
                pl.BlockSpec((KEYS, COLS), lambda k, w: (0, 0)),
                pl.BlockSpec((2, KEYS), lambda k, w: (0, 0)),
            ],
            out_specs=pl.BlockSpec((TOK, COLS), lambda k, w: (0, 0)),
            scratch_shapes=[pltpu.VMEM((TOK, COLS), jnp.float32)],
        ),
        compiler_params=pltpu.CompilerParams(vmem_limit_bytes=32 * 1024 * 1024),
        cost_estimate=pl.CostEstimate(
            flops=2 * TOK * COLS * (D + 2 * KEYS), bytes_accessed=18 << 20, transcendentals=TOK * KEYS * 4
        ),
    )(where, text, weight, scale, keys, values, bounds)


def resample(images, patch_counts, latents, latent_gain, context_gain, res_query, res_key, res_value, res_output):
    slot_count = images.shape[0]
    res_local = res_query.shape[1] // RHD
    latent_base = latents.astype(jnp.float32)
    latent_normed = layer_norm(latent_base, latent_gain.astype(jnp.float32)).astype(jnp.bfloat16)
    latent_queries = (
        jnp.dot(latent_normed, res_query, preferred_element_type=jnp.float32)
        .astype(jnp.bfloat16)
        .reshape(LAT, res_local, RHD)
    )
    context_normed = layer_norm(
        images.astype(jnp.float32), context_gain.astype(jnp.float32)
    ).astype(jnp.bfloat16)
    patch_keys = jnp.einsum(
        "cpf,fe->cpe", context_normed, res_key, preferred_element_type=jnp.float32
    ).astype(jnp.bfloat16)
    patch_values = jnp.einsum(
        "cpf,fe->cpe", context_normed, res_value, preferred_element_type=jnp.float32
    ).astype(jnp.bfloat16)
    latent_keys = jnp.dot(latent_normed, res_key, preferred_element_type=jnp.float32).astype(
        jnp.bfloat16
    )
    latent_values = jnp.dot(latent_normed, res_value, preferred_element_type=jnp.float32).astype(
        jnp.bfloat16
    )
    res_keys = jnp.concatenate(
        [patch_keys, jnp.broadcast_to(latent_keys[None], (slot_count, LAT, latent_keys.shape[1]))],
        axis=1,
    ).reshape(slot_count, PATCH + LAT, res_local, RHD)
    res_values = jnp.concatenate(
        [
            patch_values,
            jnp.broadcast_to(latent_values[None], (slot_count, LAT, latent_values.shape[1])),
        ],
        axis=1,
    ).reshape(slot_count, PATCH + LAT, res_local, RHD)
    res_scores = jnp.einsum(
        "qhd,ckhd->chqk", latent_queries, res_keys, preferred_element_type=jnp.float32
    ) * RHD ** (-0.5)
    key_rows = jnp.arange(PATCH + LAT, dtype=jnp.int32)
    patch_allowed = (key_rows[None, :] < patch_counts[:, None]) | (key_rows[None, :] >= PATCH)
    res_probs = masked_softmax(res_scores, patch_allowed[:, None, None, :])
    res_heads = (
        jnp.einsum("chqk,ckhd->cqhd", res_probs, res_values, preferred_element_type=jnp.float32)
        .astype(jnp.bfloat16)
        .reshape(slot_count, LAT, res_local * RHD)
    )
    return jnp.einsum("cqe,ef->cqf", res_heads, res_output, preferred_element_type=jnp.float32)


def local(
    text_rows,
    text_gain,
    query_weight,
    key_weight,
    value_weight,
    images,
    patch_counts,
    image_counts,
    image_spans,
    latents,
    latent_gain,
    context_gain,
    final_gain,
    res_query,
    res_key,
    res_value,
    res_output,
):
    y, z = lax.axis_index("y"), lax.axis_index("z")
    xh, xl, core = lax.axis_index("xh"), lax.axis_index("xl"), lax.axis_index("core")
    pair = y * NZ + z
    x = xh * 2 + xl

    block = jnp.concatenate([query_weight, key_weight, value_weight], axis=0)
    mine = lax.dynamic_slice_in_dim(block, xh * COLS, COLS, 1)
    other = turned(lax.dynamic_slice_in_dim(block, (1 - xh) * COLS, COLS, 1), "xh", 1, 2)
    low = jnp.where(xh == 0, mine, other)
    high = jnp.where(xh == 0, other, mine)
    part = key_weight.shape[0]
    early = low[:ROWS]
    late = jnp.concatenate(
        [
            high[:ROWS],
            low[ROWS : ROWS + part],
            high[ROWS : ROWS + part],
            low[ROWS + part :],
            high[ROWS + part :],
        ],
        axis=0,
    )
    early_all, late_all = gather_rows(early, late)

    source = text_rows.astype(jnp.float32)
    power = jnp.sum(source * source, axis=-1)
    scaled = (source * text_gain.astype(jnp.float32)).astype(jnp.bfloat16)
    text = lax.all_gather(scaled, ("xh", "xl", "core"), axis=0)

    live_slot = jnp.arange(2, dtype=jnp.int32) < image_counts[0]
    span_bounds = jnp.where(live_slot[None, :], image_spans, 0)
    small = jnp.concatenate([power, span_bounds.reshape(4).astype(jnp.float32), jnp.zeros((124,), jnp.float32)])
    small = lax.all_gather(small, ("xh", "xl", "core"), axis=0).reshape(2, 4, TOK + 128)
    power_all = jnp.sum(small[:, :, :TOK], axis=1).reshape(2 * TOK, 1)
    scale = lax.rsqrt(power_all / D + EPS_TEXT)
    own_bounds = small[:, 0, TOK : TOK + 4].reshape(2, 2, 2).transpose(1, 0, 2).reshape(2, NX)
    near = jnp.stack([next_pair(own_bounds), own_bounds], axis=1)
    near = relative(near, 2, x, NX).transpose(0, 2, 1).reshape(2, 8).astype(jnp.int32)
    bounds = jnp.repeat(near, LAT, axis=1)

    mix = resample(
        images, patch_counts, latents, latent_gain, context_gain, res_query, res_key, res_value, res_output
    ).reshape(2, 2, LAT // 2, VW)
    first = lax.dynamic_index_in_dim(mix, core, 1, keepdims=False)
    first = first + turned(lax.dynamic_index_in_dim(mix, 1 - core, 1, keepdims=False), "core", 1, 2)
    total = lax.dynamic_index_in_dim(first, xl, 0, keepdims=False)
    total = total + turned(lax.dynamic_index_in_dim(first, 1 - xl, 0, keepdims=False), "xl", 1, 2)
    base = lax.dynamic_slice_in_dim(latents, core * (LAT // 2), LAT // 2, 0).astype(jnp.float32)
    piece = layer_norm(base + total, final_gain.astype(jnp.float32)).astype(jnp.bfloat16)
    both = jnp.stack([next_pair(piece), piece])
    ring = ("xh", "xl")
    around = jnp.stack(
        [both, turned(both, ring, -1, NX), turned(both, ring, 2, NX), turned(both, ring, 1, NX)]
    )
    resampled = jnp.stack([around, turned(around, "core", 1, 2)], axis=2).reshape(KEYS, VW)

    heads_weight = absolute(absolute(late_all[:, :, ROWS:], 1, z, NZ), 0, y, NY)
    heads_weight = heads_weight.reshape(NY * NZ, 2, 2 * part, COLS)
    keys = jnp.dot(
        resampled, heads_weight[:, 0].reshape(VW, COLS), preferred_element_type=jnp.float32
    ).astype(jnp.bfloat16)
    values = jnp.dot(
        resampled, heads_weight[:, 1].reshape(VW, COLS), preferred_element_type=jnp.float32
    ).astype(jnp.bfloat16)

    weight = jnp.concatenate([early_all, late_all[:, :, :ROWS]], axis=2)
    weight = absolute(absolute(weight, 1, z, NZ), 0, y, NY).reshape(D, COLS)

    theirs = attend(1 - xh, pair, text, weight, scale, keys, values, bounds)
    received = turned(theirs, "xh", 1, 2)
    ours = attend(xh, pair, text, weight, scale, keys, values, bounds)
    return jnp.where(
        xh == 0,
        jnp.concatenate([ours, received], axis=1),
        jnp.concatenate([received, ours], axis=1),
    )


def solution(mesh):
    fine = Mesh(mesh.devices.reshape(NY, NZ, 2, 2, 2), ("y", "z", "xh", "xl", "core"))
    seq = ("y", "z", "xh")
    head = ("xl", "core")
    return jax.shard_map(
        local,
        mesh=fine,
        in_specs=(
            P(seq, head),
            P(head),
            P(seq, head),
            P(seq, head),
            P(seq, head),
            P(seq, None, None),
            P(seq),
            P(seq),
            P(None, seq),
            P(),
            P(),
            P(),
            P(),
            P(None, head),
            P(None, head),
            P(None, head),
            P(head, None),
        ),
        out_specs=P(seq, head),
        check_vma=False,
    )
```

```python
import functools

import jax
import jax.numpy as jnp
from jax import lax
from jax.experimental import pallas as pl
from jax.experimental.pallas import tpu as pltpu
from jax.sharding import Mesh, PartitionSpec as P

D = 8192
HD = 128
RHD = 96
LAT = 64
PATCH = 256
VW = 1280

EPS_TEXT = 1e-06
EPS_VISION = 1e-05
FILL = -1e30
LOG2E = 1.4426950408889634

NY, NZ, NX = 4, 8, 4
TOK = 512
COLS = 512
KEYS = 512
ROWS = 128


def layer_norm(values, gain):
    middle = jnp.mean(values, axis=-1, keepdims=True)
    centred = values - middle
    spread = jnp.mean(centred * centred, axis=-1, keepdims=True)
    return centred * lax.rsqrt(spread + EPS_VISION) * gain


def masked_softmax(scores, allowed):
    highest = jnp.max(jnp.where(allowed, scores, FILL), axis=-1, keepdims=True)
    weights = jnp.where(allowed, jnp.exp(scores - highest), 0.0)
    summed = jnp.sum(weights, axis=-1, keepdims=True)
    anything = jnp.any(allowed, axis=-1, keepdims=True)
    return (weights / jnp.where(anything, summed, 1.0)).astype(jnp.bfloat16)


def turned(x, axis, by, count):
    return lax.ppermute(x, axis, [(i, (i + by) % count) for i in range(count)])


def next_pair(x):
    return lax.ppermute(x, ("y", "z"), [(i, i + 1) for i in range(NY * NZ - 1)])


def after(x, *others):
    return lax.optimization_barrier((x, others))[0]


def flipped(x, axes):
    count = 2 ** len(axes)
    return lax.ppermute(x, axes, [(i, count - 1 - i) for i in range(count)])


AHEAD = 2


def attend_kernel(counts, fresh, *refs):
    refs = list(refs)
    take = lambda count: [refs.pop(0) for _ in range(count)]
    where_ref, gain_ref, scale_ref, bound_ref = take(4)
    if fresh:
        (rows_ref,) = take(1)
    else:
        key_ref, value_ref = take(2)
    (weight_ref,) = take(1)
    blocks = [take(count) for count in counts]
    (out_ref,) = take(1)
    if fresh:
        key_ref, value_ref = take(2)
        pair_sem, side_buf, pair_buf = refs.pop(), refs.pop(), refs.pop()
    text_buf, weight_buf, acc_ref, text_sem, weight_sem = refs

    def fetch(k):
        height = TOK // len(blocks[k])
        for j, ref in enumerate(blocks[k]):
            pltpu.make_async_copy(ref, text_buf.at[k, pl.ds(j * height, height), :], text_sem.at[k]).start()
        pltpu.make_async_copy(
            weight_ref.at[pl.ds(where_ref[1 + k] * NZ, NZ), pl.ds(0, 2 * ROWS), :], weight_buf.at[k], weight_sem.at[k]
        ).start()

    for k in range(AHEAD):
        fetch(k)
    if fresh:
        count = pair_buf.shape[1]
        pltpu.make_async_copy(weight_ref.at[:, pl.ds(2 * ROWS, count), :], pair_buf, pair_sem.at[0]).start()
    for k in range(NY):
        pltpu.make_async_copy(text_buf.at[k], text_buf.at[k], text_sem.at[k]).wait()
        pltpu.make_async_copy(weight_buf.at[k], weight_buf.at[k], weight_sem.at[k]).wait()
        if k + AHEAD < NY:
            fetch(k + AHEAD)
        part = jnp.dot(
            text_buf[k] * gain_ref[where_ref[1 + NY + k]],
            weight_buf[k].reshape(D // NY, COLS),
            preferred_element_type=jnp.float32,
        )
        acc_ref[...] = part if k == 0 else acc_ref[...] + part
        if fresh and k == 1:
            pltpu.make_async_copy(pair_buf, pair_buf, pair_sem.at[0]).wait()
            half = pair_buf.shape[1] // 2
            tall = NZ * half

            @pl.loop(0, NY)
            def _(group):
                rows = pair_buf[pl.ds(group * NZ, NZ)].astype(jnp.float32)
                start = pl.multiple_of(group * tall, tall)
                for i in range(2):
                    side = rows[:, i * half : (i + 1) * half].reshape(tall, COLS)
                    side_buf[i, pl.ds(start, tall), :] = side.astype(jnp.bfloat16)

            for i, ref in enumerate((key_ref, value_ref)):
                ref[...] = jnp.dot(
                    rows_ref[...], side_buf[i], preferred_element_type=jnp.float32
                ).astype(jnp.bfloat16)

    position = where_ref[0] + lax.broadcasted_iota(jnp.int32, (TOK, KEYS), 0)
    seen = (position >= bound_ref[0:1, :]) & (position < bound_ref[1:2, :])
    anything = jnp.any(seen, axis=-1, keepdims=True)
    hidden = jnp.where(seen, 0.0, FILL)
    for head in range(COLS // HD):
        cols = pl.ds(head * HD, HD)
        queries = (acc_ref[:, cols] * scale_ref[...]).astype(jnp.bfloat16)
        scores = lax.dot_general(
            queries, key_ref[:, cols], (((1,), (1,)), ((), ())), preferred_element_type=jnp.float32
        )
        scores = scores * (HD ** (-0.5) * LOG2E) + hidden
        highest = jnp.max(scores, axis=-1, keepdims=True)
        weights = jnp.exp2(scores - highest)
        summed = jnp.sum(weights, axis=-1, keepdims=True)
        probs = (weights * jnp.where(anything, 1.0 / summed, 0.0)).astype(jnp.bfloat16)
        out_ref[:, cols] = jnp.dot(
            probs, value_ref[:, cols], preferred_element_type=jnp.float32
        ).astype(jnp.bfloat16)


def attend(blocks, where, gain, scale, bounds, rows, weight):
    fresh = len(rows) == 1
    counts = tuple(len(refs) for refs in blocks)
    vmem = pl.BlockSpec(memory_space=pltpu.VMEM)
    anywhere = pl.BlockSpec(memory_space=pl.ANY)
    result = jax.ShapeDtypeStruct((TOK, COLS), jnp.bfloat16)
    pairs = weight.shape[1] - 2 * ROWS
    return pl.pallas_call(
        functools.partial(attend_kernel, counts, fresh),
        out_shape=[result] * (3 if fresh else 1),
        in_specs=[pl.BlockSpec(memory_space=pltpu.SMEM)] + [vmem] * (3 + len(rows)) + [anywhere] * (1 + sum(counts)),
        out_specs=[vmem] * (3 if fresh else 1),
        scratch_shapes=[
            pltpu.VMEM((NY, TOK, D // NY), jnp.bfloat16),
            pltpu.VMEM((NY, NZ, 2 * ROWS, COLS), jnp.bfloat16),
            pltpu.VMEM((TOK, COLS), jnp.float32),
            pltpu.SemaphoreType.DMA((NY,)),
            pltpu.SemaphoreType.DMA((NY,)),
        ]
        + (
            [
                pltpu.VMEM((NY * NZ, pairs, COLS), jnp.bfloat16),
                pltpu.VMEM((2, VW, COLS), jnp.bfloat16),
                pltpu.SemaphoreType.DMA((1,)),
            ]
            if fresh
            else []
        ),
        compiler_params=pltpu.CompilerParams(vmem_limit_bytes=56 * 1024 * 1024),
        cost_estimate=pl.CostEstimate(
            flops=2 * TOK * COLS * (D + 2 * KEYS), bytes_accessed=18 << 20, transcendentals=TOK * KEYS * 4
        ),
    )(where, gain, scale, bounds, *rows, weight, *(ref for refs in blocks for ref in refs))


def resample(images, patch_counts, latents, latent_gain, context_gain, res_query, res_key, res_value, res_output):
    slot_count = images.shape[0]
    res_local = res_query.shape[1] // RHD
    latent_base = latents.astype(jnp.float32)
    latent_normed = layer_norm(latent_base, latent_gain.astype(jnp.float32)).astype(jnp.bfloat16)
    latent_queries = (
        jnp.dot(latent_normed, res_query, preferred_element_type=jnp.float32)
        .astype(jnp.bfloat16)
        .reshape(LAT, res_local, RHD)
    )
    context_normed = layer_norm(
        images.astype(jnp.float32), context_gain.astype(jnp.float32)
    ).astype(jnp.bfloat16)
    patch_keys = jnp.einsum(
        "cpf,fe->cpe", context_normed, res_key, preferred_element_type=jnp.float32
    ).astype(jnp.bfloat16)
    patch_values = jnp.einsum(
        "cpf,fe->cpe", context_normed, res_value, preferred_element_type=jnp.float32
    ).astype(jnp.bfloat16)
    latent_keys = jnp.dot(latent_normed, res_key, preferred_element_type=jnp.float32).astype(
        jnp.bfloat16
    )
    latent_values = jnp.dot(latent_normed, res_value, preferred_element_type=jnp.float32).astype(
        jnp.bfloat16
    )
    res_keys = jnp.concatenate(
        [patch_keys, jnp.broadcast_to(latent_keys[None], (slot_count, LAT, latent_keys.shape[1]))],
        axis=1,
    ).reshape(slot_count, PATCH + LAT, res_local, RHD)
    res_values = jnp.concatenate(
        [
            patch_values,
            jnp.broadcast_to(latent_values[None], (slot_count, LAT, latent_values.shape[1])),
        ],
        axis=1,
    ).reshape(slot_count, PATCH + LAT, res_local, RHD)
    res_scores = jnp.einsum(
        "qhd,ckhd->chqk", latent_queries, res_keys, preferred_element_type=jnp.float32
    ) * RHD ** (-0.5)
    key_rows = jnp.arange(PATCH + LAT, dtype=jnp.int32)
    patch_allowed = (key_rows[None, :] < patch_counts[:, None]) | (key_rows[None, :] >= PATCH)
    res_probs = masked_softmax(res_scores, patch_allowed[:, None, None, :])
    res_heads = (
        jnp.einsum("chqk,ckhd->cqhd", res_probs, res_values, preferred_element_type=jnp.float32)
        .astype(jnp.bfloat16)
        .reshape(slot_count, LAT, res_local * RHD)
    )
    return jnp.einsum("cqe,ef->cqf", res_heads, res_output, preferred_element_type=jnp.float32)


def local(
    text_rows,
    text_gain,
    query_weight,
    key_weight,
    value_weight,
    images,
    patch_counts,
    image_counts,
    image_spans,
    latents,
    latent_gain,
    context_gain,
    final_gain,
    res_query,
    res_key,
    res_value,
    res_output,
):
    y, z = lax.axis_index("y"), lax.axis_index("z")
    xh, xl, core = lax.axis_index("xh"), lax.axis_index("xl"), lax.axis_index("core")
    x = xh * 2 + xl

    block = jnp.concatenate([query_weight, key_weight, value_weight], axis=0)
    mine = lax.dynamic_slice_in_dim(block, xh * COLS, COLS, 1)
    other = flipped(lax.dynamic_slice_in_dim(block, (1 - xh) * COLS, COLS, 1), ("xh",))
    low = jnp.where(xh == 0, mine, other)
    high = jnp.where(xh == 0, other, mine)
    part = key_weight.shape[0]
    pairs = jnp.concatenate([low[ROWS:], high[ROWS:]], axis=0)
    order = jnp.arange(4 * part, dtype=jnp.int32)
    block_of = jnp.asarray([0, 2, 1, 3], jnp.int32)[order // part] * part + order % part
    pairs = jnp.dot(
        (block_of[:, None] == order[None, :]).astype(jnp.bfloat16), pairs, preferred_element_type=jnp.float32
    ).astype(jnp.bfloat16)
    weight = lax.all_gather(jnp.concatenate([low[:ROWS], high[:ROWS], pairs], axis=0), ("y", "z"), axis=0)

    source = text_rows.astype(jnp.float32)
    power = jnp.sum(source * source, axis=-1)
    live_slot = jnp.arange(2, dtype=jnp.int32) < image_counts[0]
    span_bounds = jnp.where(live_slot[None, :], image_spans, 0)
    small = jnp.concatenate(
        [
            power,
            text_gain.astype(jnp.float32),
            span_bounds.reshape(4).astype(jnp.float32),
            next_pair(span_bounds.reshape(4).astype(jnp.float32)),
            jnp.zeros((120,), jnp.float32),
        ]
    )

    mix = resample(
        images, patch_counts, latents, latent_gain, context_gain, res_query, res_key, res_value, res_output
    ).reshape(2, 2, LAT // 2, VW)
    small = small[None]
    first = lax.dynamic_index_in_dim(mix, core, 1, keepdims=False)
    first = first + turned(lax.dynamic_index_in_dim(mix, 1 - core, 1, keepdims=False), "core", 1, 2)
    small = jnp.concatenate([small, flipped(small, ("core",))], axis=0)
    first, small = lax.optimization_barrier((first, small))
    total = lax.dynamic_index_in_dim(first, xl, 0, keepdims=False)
    total = total + turned(lax.dynamic_index_in_dim(first, 1 - xl, 0, keepdims=False), "xl", 1, 2)
    small = jnp.concatenate([small, flipped(small, ("xl",))], axis=0)
    total, small = lax.optimization_barrier((total, small))
    short = jnp.concatenate([jnp.sum(small[:, :TOK], axis=0), small[0, TOK + D // NY :]])
    short_other = flipped(short, ("xh",))

    text_out = after(text_rows, other, total)
    near_text, cross_text = flipped(text_out, ("xl",)), flipped(text_out, ("xh", "xl"))
    cut = TOK // 2
    text_top = flipped(cross_text[:cut], ("xl",))
    text_bottom = flipped(near_text[cut:], ("xh", "xl"))
    base = lax.dynamic_slice_in_dim(latents, core * (LAT // 2), LAT // 2, 0).astype(jnp.float32)
    piece = layer_norm(base + total, final_gain.astype(jnp.float32)).astype(jnp.bfloat16)
    both = jnp.stack([next_pair(piece), piece])

    swap = lambda rows: flipped(rows, ("core",))
    our_blocks = [[text_rows], [swap(text_rows)], [near_text], [swap(near_text)]]
    their_blocks = [[cross_text], [swap(cross_text)], [text_top, text_bottom], [swap(text_top), swap(text_bottom)]]
    scales = [lax.rsqrt(one[:TOK] / D + EPS_TEXT).reshape(TOK, 1) for one in (short, short_other)]
    gain = small[:, TOK : TOK + D // NY].astype(jnp.bfloat16).reshape(NY, 1, D // NY)
    spans = [one[TOK : TOK + 8].reshape(2, 2, 2) for one in (short, short_other)]
    spans = jnp.where(xh == 0, jnp.concatenate(spans, axis=2), jnp.concatenate(spans[::-1], axis=2))
    near = jnp.stack([spans[1], spans[0]], axis=1)
    near = jnp.take(near, x ^ jnp.arange(NX), axis=2).transpose(0, 2, 1).reshape(2, 8).astype(jnp.int32)
    bounds = jnp.repeat(near, LAT, axis=1)

    both = jnp.stack([both, flipped(both, ("xl",))])
    both = jnp.stack([both, flipped(both, ("xh",))])
    around = jnp.stack([both[0, 0], both[0, 1], both[1, 0], both[1, 1]])
    around = after(around, text_top, text_bottom)
    resampled = jnp.stack([around, turned(around, "core", 1, 2)], axis=2).reshape(KEYS, VW)

    def half(blocks, which, own_scale, others, rows):
        places = [2 * p + q for p, q in ((others, core), (others, 1 - core), (1 - others, core), (1 - others, 1 - core))]
        turns = [place ^ (2 * xl + core) for place in places]
        where = jnp.stack([(y * NZ + z) * (2 * TOK) + which * TOK, *places, *turns]).astype(jnp.int32)
        return attend(blocks, where, gain, own_scale, bounds, rows, weight)

    theirs, keys, values = half(their_blocks, 1 - xh, scales[1], 1 - xl, (resampled,))
    received = flipped(theirs, ("xh",))
    (ours,) = half(our_blocks, xh, scales[0], xl, (keys, values))
    return jnp.where(
        xh == 0,
        jnp.concatenate([ours, received], axis=1),
        jnp.concatenate([received, ours], axis=1),
    )


def solution(mesh):
    fine = Mesh(mesh.devices.reshape(NY, NZ, 2, 2, 2), ("y", "z", "xh", "xl", "core"))
    seq = ("y", "z", "xh")
    head = ("xl", "core")
    return jax.shard_map(
        local,
        mesh=fine,
        in_specs=(
            P(seq, head),
            P(head),
            P(seq, head),
            P(seq, head),
            P(seq, head),
            P(seq, None, None),
            P(seq),
            P(seq),
            P(None, seq),
            P(),
            P(),
            P(),
            P(),
            P(None, head),
            P(None, head),
            P(None, head),
            P(head, None),
        ),
        out_specs=P(seq, head),
        check_vma=False,
    )
```

```python
import functools

import jax
import jax.numpy as jnp
from jax import lax
from jax.experimental import pallas as pl
from jax.experimental.pallas import tpu as pltpu
from jax.sharding import Mesh, PartitionSpec as P

D = 8192
HD = 128
RHD = 96
LAT = 64
PATCH = 256
VW = 1280

EPS_TEXT = 1e-06
EPS_VISION = 1e-05
FILL = -1e30
LOG2E = 1.4426950408889634

NY, NZ, NX = 4, 8, 4
TOK = 512
COLS = 512
KEYS = 512
ROWS = 128


def layer_norm(values, gain):
    middle = jnp.mean(values, axis=-1, keepdims=True)
    centred = values - middle
    spread = jnp.mean(centred * centred, axis=-1, keepdims=True)
    return centred * lax.rsqrt(spread + EPS_VISION) * gain


def turned(x, axis, by, count):
    return lax.ppermute(x, axis, [(i, (i + by) % count) for i in range(count)])


def next_pair(x):
    return lax.ppermute(x, ("y", "z"), [(i, i + 1) for i in range(NY * NZ - 1)])


def after(x, *others):
    return lax.optimization_barrier((x, others))[0]


def flipped(x, axes):
    count = 2 ** len(axes)
    return lax.ppermute(x, axes, [(i, count - 1 - i) for i in range(count)])


AHEAD = 2


def attend_kernel(counts, fresh, *refs):
    refs = list(refs)
    take = lambda count: [refs.pop(0) for _ in range(count)]
    where_ref, gain_ref, scale_ref, bound_ref = take(4)
    if fresh:
        (rows_ref,) = take(1)
    else:
        key_ref, value_ref = take(2)
    (weight_ref,) = take(1)
    blocks = [take(count) for count in counts]
    (out_ref,) = take(1)
    if fresh:
        key_ref, value_ref = take(2)
        pair_sem, side_buf, pair_buf = refs.pop(), refs.pop(), refs.pop()
    text_buf, weight_buf, acc_ref, text_sem, weight_sem = refs

    def fetch(k):
        height = TOK // len(blocks[k])
        for j, ref in enumerate(blocks[k]):
            pltpu.make_async_copy(ref, text_buf.at[k, pl.ds(j * height, height), :], text_sem.at[k]).start()
        pltpu.make_async_copy(
            weight_ref.at[pl.ds(where_ref[1 + k] * NZ, NZ), pl.ds(0, 2 * ROWS), :], weight_buf.at[k], weight_sem.at[k]
        ).start()

    for k in range(AHEAD):
        fetch(k)
    if fresh:
        count = pair_buf.shape[1]
        pltpu.make_async_copy(weight_ref.at[:, pl.ds(2 * ROWS, count), :], pair_buf, pair_sem.at[0]).start()
    for k in range(NY):
        pltpu.make_async_copy(text_buf.at[k], text_buf.at[k], text_sem.at[k]).wait()
        pltpu.make_async_copy(weight_buf.at[k], weight_buf.at[k], weight_sem.at[k]).wait()
        if k + AHEAD < NY:
            fetch(k + AHEAD)
        part = jnp.dot(
            text_buf[k] * gain_ref[where_ref[1 + NY + k]],
            weight_buf[k].reshape(D // NY, COLS),
            preferred_element_type=jnp.float32,
        )
        acc_ref[...] = part if k == 0 else acc_ref[...] + part
        if fresh and k == 1:
            pltpu.make_async_copy(pair_buf, pair_buf, pair_sem.at[0]).wait()
            half = pair_buf.shape[1] // 2
            tall = NZ * half

            @pl.loop(0, NY)
            def _(group):
                rows = pair_buf[pl.ds(group * NZ, NZ)].astype(jnp.float32)
                start = pl.multiple_of(group * tall, tall)
                for i in range(2):
                    side = rows[:, i * half : (i + 1) * half].reshape(tall, COLS)
                    side_buf[i, pl.ds(start, tall), :] = side.astype(jnp.bfloat16)

            for i, ref in enumerate((key_ref, value_ref)):
                ref[...] = jnp.dot(
                    rows_ref[...], side_buf[i], preferred_element_type=jnp.float32
                ).astype(jnp.bfloat16)

    position = where_ref[0] + lax.broadcasted_iota(jnp.int32, (TOK, KEYS), 0)
    seen = (position >= bound_ref[0:1, :]) & (position < bound_ref[1:2, :])
    anything = jnp.any(seen, axis=-1, keepdims=True)
    hidden = jnp.where(seen, 0.0, FILL)
    for head in range(COLS // HD):
        cols = pl.ds(head * HD, HD)
        queries = (acc_ref[:, cols] * scale_ref[...]).astype(jnp.bfloat16)
        scores = lax.dot_general(
            queries, key_ref[:, cols], (((1,), (1,)), ((), ())), preferred_element_type=jnp.float32
        )
        scores = scores * (HD ** (-0.5) * LOG2E) + hidden
        highest = jnp.max(scores, axis=-1, keepdims=True)
        weights = jnp.exp2(scores - highest)
        summed = jnp.sum(weights, axis=-1, keepdims=True)
        probs = (weights * jnp.where(anything, 1.0 / summed, 0.0)).astype(jnp.bfloat16)
        out_ref[:, cols] = jnp.dot(
            probs, value_ref[:, cols], preferred_element_type=jnp.float32
        ).astype(jnp.bfloat16)


def attend(blocks, where, gain, scale, bounds, rows, weight):
    fresh = len(rows) == 1
    counts = tuple(len(refs) for refs in blocks)
    vmem = pl.BlockSpec(memory_space=pltpu.VMEM)
    anywhere = pl.BlockSpec(memory_space=pl.ANY)
    result = jax.ShapeDtypeStruct((TOK, COLS), jnp.bfloat16)
    pairs = weight.shape[1] - 2 * ROWS
    return pl.pallas_call(
        functools.partial(attend_kernel, counts, fresh),
        out_shape=[result] * (3 if fresh else 1),
        in_specs=[pl.BlockSpec(memory_space=pltpu.SMEM)] + [vmem] * (3 + len(rows)) + [anywhere] * (1 + sum(counts)),
        out_specs=[vmem] * (3 if fresh else 1),
        scratch_shapes=[
            pltpu.VMEM((NY, TOK, D // NY), jnp.bfloat16),
            pltpu.VMEM((NY, NZ, 2 * ROWS, COLS), jnp.bfloat16),
            pltpu.VMEM((TOK, COLS), jnp.float32),
            pltpu.SemaphoreType.DMA((NY,)),
            pltpu.SemaphoreType.DMA((NY,)),
        ]
        + (
            [
                pltpu.VMEM((NY * NZ, pairs, COLS), jnp.bfloat16),
                pltpu.VMEM((2, VW, COLS), jnp.bfloat16),
                pltpu.SemaphoreType.DMA((1,)),
            ]
            if fresh
            else []
        ),
        compiler_params=pltpu.CompilerParams(vmem_limit_bytes=56 * 1024 * 1024),
        cost_estimate=pl.CostEstimate(
            flops=2 * TOK * COLS * (D + 2 * KEYS), bytes_accessed=18 << 20, transcendentals=TOK * KEYS * 4
        ),
    )(where, gain, scale, bounds, *rows, weight, *(ref for refs in blocks for ref in refs))


def resample_kernel(
    count_ref, image_ref, latent_ref, latent_gain_ref, context_gain_ref, query_ref, key_ref, value_ref, output_ref, out_ref
):
    latent_normed = layer_norm(
        latent_ref[...].astype(jnp.float32), latent_gain_ref[...].astype(jnp.float32)
    ).astype(jnp.bfloat16)

    def project(rows, weight_ref):
        return jnp.dot(rows, weight_ref[...], preferred_element_type=jnp.float32).astype(jnp.bfloat16)

    width = query_ref.shape[1]
    heads = width // RHD
    column = lax.broadcasted_iota(jnp.int32, (LAT, width), 1)
    masks = [(column >= h * RHD) & (column < (h + 1) * RHD) for h in range(heads)]
    latent_queries = project(latent_normed, query_ref).astype(jnp.float32)
    queries = jnp.concatenate([jnp.where(mask, latent_queries, 0.0) for mask in masks], axis=0).astype(jnp.bfloat16)
    for slot in range(image_ref.shape[0]):
        context = layer_norm(
            image_ref[slot].astype(jnp.float32), context_gain_ref[...].astype(jnp.float32)
        ).astype(jnp.bfloat16)
        joined = jnp.concatenate([context, latent_normed], axis=0)
        keys, values = project(joined, key_ref), project(joined, value_ref)
        scores = lax.dot_general(
            queries, keys, (((1,), (1,)), ((), ())), preferred_element_type=jnp.float32
        ) * RHD ** (-0.5)
        row = lax.broadcasted_iota(jnp.int32, scores.shape, 1)
        allowed = (row < count_ref[slot]) | (row >= PATCH)
        scores = jnp.where(allowed, scores, FILL)
        weights = jnp.exp(scores - jnp.max(scores, axis=-1, keepdims=True))
        probs = (weights / jnp.sum(weights, axis=-1, keepdims=True)).astype(jnp.bfloat16)
        mixed = jnp.dot(probs, values, preferred_element_type=jnp.float32)
        res_heads = sum(
            jnp.where(mask, mixed[h * LAT : (h + 1) * LAT], 0.0) for h, mask in enumerate(masks)
        ).astype(jnp.bfloat16)
        out_ref[slot] = jnp.dot(res_heads, output_ref[...], preferred_element_type=jnp.float32)


def resample(images, patch_counts, latents, latent_gain, context_gain, res_query, res_key, res_value, res_output):
    vmem = pl.BlockSpec(memory_space=pltpu.VMEM)
    return pl.pallas_call(
        resample_kernel,
        out_shape=jax.ShapeDtypeStruct((images.shape[0], LAT, VW), jnp.float32),
        in_specs=[pl.BlockSpec(memory_space=pltpu.SMEM)] + [vmem] * 8,
        out_specs=vmem,
        compiler_params=pltpu.CompilerParams(vmem_limit_bytes=40 * 1024 * 1024),
        cost_estimate=pl.CostEstimate(flops=30 << 30, bytes_accessed=8 << 20, transcendentals=1 << 18),
    )(
        patch_counts, images, latents, latent_gain[None], context_gain[None], res_query, res_key, res_value, res_output
    )


def local(
    text_rows,
    text_gain,
    query_weight,
    key_weight,
    value_weight,
    images,
    patch_counts,
    image_counts,
    image_spans,
    latents,
    latent_gain,
    context_gain,
    final_gain,
    res_query,
    res_key,
    res_value,
    res_output,
):
    y, z = lax.axis_index("y"), lax.axis_index("z")
    xh, xl, core = lax.axis_index("xh"), lax.axis_index("xl"), lax.axis_index("core")
    x = xh * 2 + xl

    block = jnp.concatenate([query_weight, key_weight, value_weight], axis=0)
    mine = lax.dynamic_slice_in_dim(block, xh * COLS, COLS, 1)
    other = flipped(lax.dynamic_slice_in_dim(block, (1 - xh) * COLS, COLS, 1), ("xh",))
    low = jnp.where(xh == 0, mine, other)
    high = jnp.where(xh == 0, other, mine)
    part = key_weight.shape[0]
    pairs = jnp.concatenate([low[ROWS:], high[ROWS:]], axis=0)
    order = jnp.arange(4 * part, dtype=jnp.int32)
    block_of = jnp.asarray([0, 2, 1, 3], jnp.int32)[order // part] * part + order % part
    pairs = jnp.dot(
        (block_of[:, None] == order[None, :]).astype(jnp.bfloat16), pairs, preferred_element_type=jnp.float32
    ).astype(jnp.bfloat16)
    weight = lax.all_gather(jnp.concatenate([low[:ROWS], high[:ROWS], pairs], axis=0), ("y", "z"), axis=0)

    source = text_rows.astype(jnp.float32)
    power = jnp.sum(source * source, axis=-1)
    live_slot = jnp.arange(2, dtype=jnp.int32) < image_counts[0]
    span_bounds = jnp.where(live_slot[None, :], image_spans, 0)
    small = jnp.concatenate(
        [
            power,
            text_gain.astype(jnp.float32),
            span_bounds.reshape(4).astype(jnp.float32),
            next_pair(span_bounds.reshape(4).astype(jnp.float32)),
            jnp.zeros((120,), jnp.float32),
        ]
    )

    mix = resample(
        images, patch_counts, latents, latent_gain, context_gain, res_query, res_key, res_value, res_output
    ).reshape(2, 2, LAT // 2, VW)
    small = small[None]
    first = lax.dynamic_index_in_dim(mix, core, 1, keepdims=False)
    first = first + turned(lax.dynamic_index_in_dim(mix, 1 - core, 1, keepdims=False), "core", 1, 2)
    small = jnp.concatenate([small, flipped(small, ("core",))], axis=0)
    text_out = after(text_rows, other)
    near_text, cross_text = flipped(text_out, ("xl",)), flipped(text_out, ("xh", "xl"))
    near_text, cross_text, first, small = lax.optimization_barrier((near_text, cross_text, first, small))
    cut = TOK // 2
    text_top = flipped(cross_text[:cut], ("xl",))
    text_bottom = flipped(near_text[cut:], ("xh", "xl"))
    total = lax.dynamic_index_in_dim(first, xl, 0, keepdims=False)
    total = total + turned(lax.dynamic_index_in_dim(first, 1 - xl, 0, keepdims=False), "xl", 1, 2)
    small = jnp.concatenate([small, flipped(small, ("xl",))], axis=0)
    text_top, text_bottom, total, small = lax.optimization_barrier((text_top, text_bottom, total, small))
    short = jnp.concatenate([jnp.sum(small[:, :TOK], axis=0), small[0, TOK + D // NY :]])
    short_other = flipped(short, ("xh",))

    base = lax.dynamic_slice_in_dim(latents, core * (LAT // 2), LAT // 2, 0).astype(jnp.float32)
    piece = layer_norm(base + total, final_gain.astype(jnp.float32)).astype(jnp.bfloat16)
    both = jnp.stack([next_pair(piece), piece])

    swap = lambda rows: flipped(rows, ("core",))
    our_blocks = [[text_rows], [swap(text_rows)], [near_text], [swap(near_text)]]
    their_blocks = [[cross_text], [swap(cross_text)], [text_top, text_bottom], [swap(text_top), swap(text_bottom)]]
    scales = [lax.rsqrt(one[:TOK] / D + EPS_TEXT).reshape(TOK, 1) for one in (short, short_other)]
    gain = small[:, TOK : TOK + D // NY].astype(jnp.bfloat16).reshape(NY, 1, D // NY)
    spans = [one[TOK : TOK + 8].reshape(2, 2, 2) for one in (short, short_other)]
    spans = jnp.where(xh == 0, jnp.concatenate(spans, axis=2), jnp.concatenate(spans[::-1], axis=2))
    near = jnp.stack([spans[1], spans[0]], axis=1)
    near = jnp.take(near, x ^ jnp.arange(NX), axis=2).transpose(0, 2, 1).reshape(2, 8).astype(jnp.int32)
    bounds = jnp.repeat(near, LAT, axis=1)

    both = jnp.stack([both, flipped(both, ("xl",))])
    both = jnp.stack([both, flipped(both, ("xh",))])
    around = jnp.stack([both[0, 0], both[0, 1], both[1, 0], both[1, 1]])
    resampled = jnp.stack([around, turned(around, "core", 1, 2)], axis=2).reshape(KEYS, VW)

    def half(blocks, which, own_scale, others, rows):
        places = [2 * p + q for p, q in ((others, core), (others, 1 - core), (1 - others, core), (1 - others, 1 - core))]
        turns = [place ^ (2 * xl + core) for place in places]
        where = jnp.stack([(y * NZ + z) * (2 * TOK) + which * TOK, *places, *turns]).astype(jnp.int32)
        return attend(blocks, where, gain, own_scale, bounds, rows, weight)

    theirs, keys, values = half(their_blocks, 1 - xh, scales[1], 1 - xl, (resampled,))
    received = flipped(theirs, ("xh",))
    (ours,) = half(our_blocks, xh, scales[0], xl, (keys, values))
    return jnp.where(
        xh == 0,
        jnp.concatenate([ours, received], axis=1),
        jnp.concatenate([received, ours], axis=1),
    )


def solution(mesh):
    fine = Mesh(mesh.devices.reshape(NY, NZ, 2, 2, 2), ("y", "z", "xh", "xl", "core"))
    seq = ("y", "z", "xh")
    head = ("xl", "core")
    return jax.shard_map(
        local,
        mesh=fine,
        in_specs=(
            P(seq, head),
            P(head),
            P(seq, head),
            P(seq, head),
            P(seq, head),
            P(seq, None, None),
            P(seq),
            P(seq),
            P(None, seq),
            P(),
            P(),
            P(),
            P(),
            P(None, head),
            P(None, head),
            P(None, head),
            P(head, None),
        ),
        out_specs=P(seq, head),
        check_vma=False,
    )
```

```python
import functools

import jax
import jax.numpy as jnp
from jax import lax
from jax.experimental import pallas as pl
from jax.experimental.pallas import tpu as pltpu
from jax.sharding import Mesh, PartitionSpec as P

D = 8192
HD = 128
RHD = 96
LAT = 64
PATCH = 256
VW = 1280

EPS_TEXT = 1e-06
EPS_VISION = 1e-05
FILL = -1e30
LOG2E = 1.4426950408889634

NY, NZ, NX = 4, 8, 4
TOK = 512
COLS = 512
KEYS = 512
ROWS = 128


def layer_norm(values, gain):
    middle = jnp.mean(values, axis=-1, keepdims=True)
    centred = values - middle
    spread = jnp.mean(centred * centred, axis=-1, keepdims=True)
    return centred * lax.rsqrt(spread + EPS_VISION) * gain


def turned(x, axis, by, count):
    return lax.ppermute(x, axis, [(i, (i + by) % count) for i in range(count)])


def next_pair(x):
    return lax.ppermute(x, ("y", "z"), [(i, i + 1) for i in range(NY * NZ - 1)])


def after(x, *others):
    return lax.optimization_barrier((x, others))[0]


def flipped(x, axes):
    count = 2 ** len(axes)
    return lax.ppermute(x, axes, [(i, count - 1 - i) for i in range(count)])


CHUNKS = 8
DEEP = D // CHUNKS
WIDE = DEEP // (2 * ROWS)


def attend_kernel(counts, fresh, *refs):
    refs = list(refs)
    take = lambda count: [refs.pop(0) for _ in range(count)]
    where_ref, gain_ref, scale_ref, bound_ref = take(4)
    if fresh:
        (rows_ref,) = take(1)
    else:
        key_ref, value_ref = take(2)
    (weight_ref,) = take(1)
    blocks = [take(count) for count in counts]
    (out_ref,) = take(1)
    if fresh:
        key_ref, value_ref = take(2)
        pair_sem, side_buf, pair_buf = refs.pop(), refs.pop(), refs.pop()
    text_buf, weight_buf, acc_ref, text_sem, weight_sem = refs

    def fetch(chunk):
        k, i = divmod(chunk, CHUNKS // NY)
        height = TOK // len(blocks[k])
        for j, ref in enumerate(blocks[k]):
            pltpu.make_async_copy(
                ref.at[:, pl.ds(i * DEEP, DEEP)],
                text_buf.at[chunk, pl.ds(j * height, height), :],
                text_sem.at[chunk],
            ).start()
        pltpu.make_async_copy(
            weight_ref.at[pl.ds(i * WIDE, WIDE), where_ref[1 + k], pl.ds(0, 2 * ROWS), :],
            weight_buf.at[chunk],
            weight_sem.at[chunk],
        ).start()

    fetch(0)
    if fresh:
        count = pair_buf.shape[2]
        pltpu.make_async_copy(weight_ref.at[:, :, pl.ds(2 * ROWS, count), :], pair_buf, pair_sem.at[0]).start()
    ahead = 4 if fresh else CHUNKS
    for chunk in range(1, ahead):
        fetch(chunk)
    for chunk in range(CHUNKS):
        k, i = divmod(chunk, CHUNKS // NY)
        pltpu.make_async_copy(text_buf.at[chunk], text_buf.at[chunk], text_sem.at[chunk]).wait()
        pltpu.make_async_copy(weight_buf.at[chunk], weight_buf.at[chunk], weight_sem.at[chunk]).wait()
        if chunk + ahead < CHUNKS:
            fetch(chunk + ahead)
        part = jnp.dot(
            text_buf[chunk] * gain_ref[where_ref[1 + NY + k], :, pl.ds(i * DEEP, DEEP)],
            weight_buf[chunk].reshape(DEEP, COLS),
            preferred_element_type=jnp.float32,
        )
        acc_ref[...] = part if chunk == 0 else acc_ref[...] + part
        if fresh and chunk == 3:
            pltpu.make_async_copy(pair_buf, pair_buf, pair_sem.at[0]).wait()
            half = pair_buf.shape[2] // 2
            tall = NZ * half

            @pl.loop(0, NY)
            def _(group):
                rows = pair_buf[:, group].astype(jnp.float32)
                start = pl.multiple_of(group * tall, tall)
                for i in range(2):
                    side = rows[:, i * half : (i + 1) * half].reshape(tall, COLS)
                    side_buf[i, pl.ds(start, tall), :] = side.astype(jnp.bfloat16)

            for i, ref in enumerate((key_ref, value_ref)):
                ref[...] = jnp.dot(
                    rows_ref[...], side_buf[i], preferred_element_type=jnp.float32
                ).astype(jnp.bfloat16)

    position = where_ref[0] + lax.broadcasted_iota(jnp.int32, (TOK, KEYS), 0)
    seen = (position >= bound_ref[0:1, :]) & (position < bound_ref[1:2, :])
    anything = jnp.any(seen, axis=-1, keepdims=True)
    hidden = jnp.where(seen, 0.0, FILL)
    for head in range(COLS // HD):
        cols = pl.ds(head * HD, HD)
        queries = (acc_ref[:, cols] * scale_ref[pl.ds(TOK if fresh else 0, TOK), :]).astype(jnp.bfloat16)
        scores = lax.dot_general(
            queries, key_ref[:, cols], (((1,), (1,)), ((), ())), preferred_element_type=jnp.float32
        )
        scores = scores * (HD ** (-0.5) * LOG2E) + hidden
        highest = jnp.max(scores, axis=-1, keepdims=True)
        weights = jnp.exp2(scores - highest)
        summed = jnp.sum(weights, axis=-1, keepdims=True)
        probs = (weights * jnp.where(anything, 1.0 / summed, 0.0)).astype(jnp.bfloat16)
        out_ref[:, cols] = jnp.dot(
            probs, value_ref[:, cols], preferred_element_type=jnp.float32
        ).astype(jnp.bfloat16)


def attend(blocks, where, gain, scale, bounds, rows, weight):
    fresh = len(rows) == 1
    counts = tuple(len(refs) for refs in blocks)
    vmem = pl.BlockSpec(memory_space=pltpu.VMEM)
    anywhere = pl.BlockSpec(memory_space=pl.ANY)
    result = jax.ShapeDtypeStruct((TOK, COLS), jnp.bfloat16)
    pairs = weight.shape[2] - 2 * ROWS
    return pl.pallas_call(
        functools.partial(attend_kernel, counts, fresh),
        out_shape=[result] * (3 if fresh else 1),
        in_specs=[pl.BlockSpec(memory_space=pltpu.SMEM)] + [vmem] * (3 + len(rows)) + [anywhere] * (1 + sum(counts)),
        out_specs=[vmem] * (3 if fresh else 1),
        scratch_shapes=[
            pltpu.VMEM((CHUNKS, TOK, DEEP), jnp.bfloat16),
            pltpu.VMEM((CHUNKS, WIDE, 2 * ROWS, COLS), jnp.bfloat16),
            pltpu.VMEM((TOK, COLS), jnp.float32),
            pltpu.SemaphoreType.DMA((CHUNKS,)),
            pltpu.SemaphoreType.DMA((CHUNKS,)),
        ]
        + (
            [
                pltpu.VMEM((NZ, NY, pairs, COLS), jnp.bfloat16),
                pltpu.VMEM((2, VW, COLS), jnp.bfloat16),
                pltpu.SemaphoreType.DMA((1,)),
            ]
            if fresh
            else []
        ),
        compiler_params=pltpu.CompilerParams(vmem_limit_bytes=62 * 1024 * 1024),
        cost_estimate=pl.CostEstimate(
            flops=2 * TOK * COLS * (D + 2 * KEYS), bytes_accessed=18 << 20, transcendentals=TOK * KEYS * 4
        ),
    )(where, gain, scale, bounds, *rows, weight, *(ref for refs in blocks for ref in refs))


def resample_kernel(
    count_ref, image_ref, latent_ref, latent_gain_ref, context_gain_ref, query_ref, key_ref, value_ref, output_ref, out_ref
):
    latent_normed = layer_norm(
        latent_ref[...].astype(jnp.float32), latent_gain_ref[...].astype(jnp.float32)
    ).astype(jnp.bfloat16)

    def project(rows, weight_ref):
        return jnp.dot(rows, weight_ref[...], preferred_element_type=jnp.float32).astype(jnp.bfloat16)

    width = query_ref.shape[1]
    heads = width // RHD
    column = lax.broadcasted_iota(jnp.int32, (LAT, width), 1)
    masks = [(column >= h * RHD) & (column < (h + 1) * RHD) for h in range(heads)]
    latent_queries = project(latent_normed, query_ref).astype(jnp.float32)
    queries = jnp.concatenate([jnp.where(mask, latent_queries, 0.0) for mask in masks], axis=0).astype(jnp.bfloat16)
    for slot in range(image_ref.shape[0]):
        context = layer_norm(
            image_ref[slot].astype(jnp.float32), context_gain_ref[...].astype(jnp.float32)
        ).astype(jnp.bfloat16)
        joined = jnp.concatenate([context, latent_normed], axis=0)
        keys, values = project(joined, key_ref), project(joined, value_ref)
        scores = lax.dot_general(
            queries, keys, (((1,), (1,)), ((), ())), preferred_element_type=jnp.float32
        ) * RHD ** (-0.5)
        row = lax.broadcasted_iota(jnp.int32, scores.shape, 1)
        allowed = (row < count_ref[slot]) | (row >= PATCH)
        scores = jnp.where(allowed, scores, FILL)
        weights = jnp.exp(scores - jnp.max(scores, axis=-1, keepdims=True))
        probs = (weights / jnp.sum(weights, axis=-1, keepdims=True)).astype(jnp.bfloat16)
        mixed = jnp.dot(probs, values, preferred_element_type=jnp.float32)
        res_heads = sum(
            jnp.where(mask, mixed[h * LAT : (h + 1) * LAT], 0.0) for h, mask in enumerate(masks)
        ).astype(jnp.bfloat16)
        out_ref[slot] = jnp.dot(res_heads, output_ref[...], preferred_element_type=jnp.float32)


def resample(images, patch_counts, latents, latent_gain, context_gain, res_query, res_key, res_value, res_output):
    vmem = pl.BlockSpec(memory_space=pltpu.VMEM)
    return pl.pallas_call(
        resample_kernel,
        out_shape=jax.ShapeDtypeStruct((images.shape[0], LAT, VW), jnp.float32),
        in_specs=[pl.BlockSpec(memory_space=pltpu.SMEM)] + [vmem] * 8,
        out_specs=vmem,
        compiler_params=pltpu.CompilerParams(vmem_limit_bytes=40 * 1024 * 1024),
        cost_estimate=pl.CostEstimate(flops=30 << 30, bytes_accessed=8 << 20, transcendentals=1 << 18),
    )(
        patch_counts, images, latents, latent_gain[None], context_gain[None], res_query, res_key, res_value, res_output
    )


def local(
    text_rows,
    text_gain,
    query_weight,
    key_weight,
    value_weight,
    images,
    patch_counts,
    image_counts,
    image_spans,
    latents,
    latent_gain,
    context_gain,
    final_gain,
    res_query,
    res_key,
    res_value,
    res_output,
):
    y, z = lax.axis_index("y"), lax.axis_index("z")
    xh, xl, core = lax.axis_index("xh"), lax.axis_index("xl"), lax.axis_index("core")
    x = xh * 2 + xl

    def side(which):
        parts = (query_weight, key_weight, value_weight)
        return jnp.concatenate([lax.dynamic_slice_in_dim(one, which * COLS, COLS, 1) for one in parts], axis=0)

    mine, other = side(xh), flipped(side(1 - xh), ("xh",))
    low = jnp.where(xh == 0, mine, other)
    high = jnp.where(xh == 0, other, mine)
    part = key_weight.shape[0]
    pairs = jnp.concatenate([low[ROWS:], high[ROWS:]], axis=0)
    order = jnp.arange(4 * part, dtype=jnp.int32)
    block_of = jnp.asarray([0, 2, 1, 3], jnp.int32)[order // part] * part + order % part
    pairs = jnp.dot(
        (block_of[:, None] == order[None, :]).astype(jnp.bfloat16), pairs, preferred_element_type=jnp.float32
    ).astype(jnp.bfloat16)
    weight = lax.all_gather(jnp.concatenate([low[:ROWS], high[:ROWS], pairs], axis=0), ("z", "y"), axis=0)
    weight = weight.reshape(NZ, NY, -1, COLS)

    source = text_rows.astype(jnp.float32)
    power = jnp.sum(source * source, axis=-1)
    live_slot = jnp.arange(2, dtype=jnp.int32) < image_counts[0]
    span_bounds = jnp.where(live_slot[None, :], image_spans, 0)
    mix = resample(
        images, patch_counts, latents, latent_gain, context_gain, res_query, res_key, res_value, res_output
    ).reshape(2, 2, LAT // 2, VW)
    small = jnp.concatenate(
        [
            power,
            text_gain.astype(jnp.float32),
            span_bounds.reshape(4).astype(jnp.float32),
            next_pair(after(span_bounds.reshape(4).astype(jnp.float32), mix)),
            jnp.zeros((4 * VW - TOK - D // NY - 8,), jnp.float32),
        ]
    ).reshape(1, 4, VW)
    text_out = after(text_rows, other)
    cut = TOK // 2
    halves = (text_out[:cut], text_out[cut:])
    near_bottom, cross_top = flipped(halves[1], ("xl",)), flipped(halves[0], ("xh", "xl"))
    cross_top, near_bottom, mix = lax.optimization_barrier((cross_top, near_bottom, mix))
    sent = jnp.concatenate(
        [lax.dynamic_index_in_dim(mix, 1 - core, 1, keepdims=False).reshape(LAT, VW), small[0]], axis=0
    )
    got = flipped(sent, ("core",))
    first = lax.dynamic_index_in_dim(mix, core, 1, keepdims=False) + got[:LAT].reshape(2, LAT // 2, VW)
    small = jnp.stack([small[0], got[LAT:]])
    sent = jnp.concatenate([lax.dynamic_index_in_dim(first, 1 - xl, 0, keepdims=False), small.reshape(8, VW)], axis=0)
    got = flipped(sent, ("xl",))
    small = small.reshape(2, 4 * VW)
    short = jnp.concatenate([jnp.sum(small[:, :TOK], axis=0), small[0, TOK + D // NY :][:128]])
    cross_top, near_bottom, *halves, got = lax.optimization_barrier((cross_top, near_bottom, *halves, got))
    near_text = [flipped(halves[0], ("xl",)), near_bottom]
    cross_text = [cross_top, flipped(halves[1], ("xh", "xl"))]
    far_text = [flipped(cross_top, ("xl",)), flipped(near_bottom, ("xh", "xl"))]
    total = lax.dynamic_index_in_dim(first, xl, 0, keepdims=False) + got[: LAT // 2]
    small = jnp.concatenate([small, got[LAT // 2 :].reshape(2, 4 * VW)], axis=0)

    base = lax.dynamic_slice_in_dim(latents, core * (LAT // 2), LAT // 2, 0).astype(jnp.float32)
    piece = layer_norm(base + total, final_gain.astype(jnp.float32)).astype(jnp.bfloat16)
    both = jnp.stack([next_pair(piece), piece])
    near_text[0], cross_text[1], *far_text, both = lax.optimization_barrier(
        (near_text[0], cross_text[1], *far_text, both)
    )
    both, short_cross, short_far = lax.optimization_barrier(
        (jnp.stack([both, flipped(both, ("xl",))]), flipped(short, ("xh", "xl")), flipped(short, ("xh",)))
    )

    swap = lambda rows: [flipped(one, ("core",)) for one in rows]
    our_blocks = [[text_rows], swap([text_rows]), near_text, swap(near_text)]
    their_blocks = [cross_text, swap(cross_text), far_text, swap(far_text)]
    power = jnp.concatenate([jnp.sum(small[:, :TOK], axis=0), short_cross[:TOK] + short_far[:TOK]])
    scale = lax.rsqrt(power / D + EPS_TEXT).reshape(2 * TOK, 1)
    gain = small[:, TOK : TOK + D // NY].astype(jnp.bfloat16).reshape(NY, 1, D // NY)
    spans = [one[TOK : TOK + 8].reshape(2, 2, 2) for one in (short, short_far)]
    spans = jnp.where(xh == 0, jnp.concatenate(spans, axis=2), jnp.concatenate(spans[::-1], axis=2))
    near = jnp.stack([spans[1], spans[0]], axis=1)
    near = jnp.take(near, x ^ jnp.arange(NX), axis=2).transpose(0, 2, 1).reshape(2, 8).astype(jnp.int32)
    bounds = jnp.tile(jnp.repeat(near, LAT // 2, axis=1), (1, 2))

    both = jnp.stack([both, flipped(both, ("xh",))])
    around = jnp.stack([both[0, 0], both[0, 1], both[1, 0], both[1, 1]])
    resampled = jnp.concatenate([around, turned(around, "core", 1, 2)], axis=0).reshape(KEYS, VW)

    def half(blocks, which, others, rows):
        places = [2 * p + q for p, q in ((others, core), (others, 1 - core), (1 - others, core), (1 - others, 1 - core))]
        turns = [place ^ (2 * xl + core) for place in places]
        where = jnp.stack([(y * NZ + z) * (2 * TOK) + which * TOK, *places, *turns]).astype(jnp.int32)
        return attend(blocks, where, gain, scale, bounds, rows, weight)

    theirs, keys, values = half(their_blocks, 1 - xh, 1 - xl, (resampled,))
    received = flipped(theirs, ("xh",))
    (ours,) = half(our_blocks, xh, xl, (keys, values))
    return jnp.where(
        xh == 0,
        jnp.concatenate([ours, received], axis=1),
        jnp.concatenate([received, ours], axis=1),
    )


def solution(mesh):
    fine = Mesh(mesh.devices.reshape(NY, NZ, 2, 2, 2), ("y", "z", "xh", "xl", "core"))
    seq = ("y", "z", "xh")
    head = ("xl", "core")
    return jax.shard_map(
        local,
        mesh=fine,
        in_specs=(
            P(seq, head),
            P(head),
            P(seq, head),
            P(seq, head),
            P(seq, head),
            P(seq, None, None),
            P(seq),
            P(seq),
            P(None, seq),
            P(),
            P(),
            P(),
            P(),
            P(None, head),
            P(None, head),
            P(None, head),
            P(head, None),
        ),
        out_specs=P(seq, head),
        check_vma=False,
    )
```

```python
import functools

import jax
import jax.numpy as jnp
from jax import lax
from jax.experimental import pallas as pl
from jax.experimental.pallas import tpu as pltpu
from jax.sharding import Mesh, PartitionSpec as P

D = 8192
HD = 128
RHD = 96
LAT = 64
PATCH = 256
VW = 1280

EPS_TEXT = 1e-06
EPS_VISION = 1e-05
FILL = -1e30
LOG2E = 1.4426950408889634

NY, NZ, NX = 4, 8, 4
TOK = 512
COLS = 512
KEYS = 512
ROWS = 128


def layer_norm(values, gain):
    middle = jnp.mean(values, axis=-1, keepdims=True)
    centred = values - middle
    spread = jnp.mean(centred * centred, axis=-1, keepdims=True)
    return centred * lax.rsqrt(spread + EPS_VISION) * gain


def turned(x, axis, by, count):
    return lax.ppermute(x, axis, [(i, (i + by) % count) for i in range(count)])


def next_pair(x):
    return lax.ppermute(x, ("y", "z"), [(i, i + 1) for i in range(NY * NZ - 1)])


def after(x, *others):
    return lax.optimization_barrier((x, others))[0]


def flipped(x, axes):
    count = 2 ** len(axes)
    return lax.ppermute(x, axes, [(i, count - 1 - i) for i in range(count)])


CHUNKS = 8
DEEP = D // CHUNKS
WIDE = DEEP // (2 * ROWS)


def attend_kernel(counts, fresh, *refs):
    refs = list(refs)
    take = lambda count: [refs.pop(0) for _ in range(count)]
    where_ref, gain_ref, scale_ref, bound_ref = take(4)
    if fresh:
        (rows_ref,) = take(1)
    else:
        key_ref, value_ref = take(2)
    (weight_ref,) = take(1)
    blocks = [take(count) for count in counts]
    (out_ref,) = take(1)
    if fresh:
        key_ref, value_ref = take(2)
        pair_sem, side_buf, pair_buf = refs.pop(), refs.pop(), refs.pop()
    text_buf, weight_buf, acc_ref, text_sem, weight_sem = refs

    def fetch(chunk):
        k, i = divmod(chunk, CHUNKS // NY)
        height = TOK // len(blocks[k])
        for j, ref in enumerate(blocks[k]):
            pltpu.make_async_copy(
                ref.at[:, pl.ds(i * DEEP, DEEP)],
                text_buf.at[chunk, pl.ds(j * height, height), :],
                text_sem.at[chunk],
            ).start()
        pltpu.make_async_copy(
            weight_ref.at[pl.ds(i * WIDE, WIDE), where_ref[1 + k], pl.ds(0, 2 * ROWS), :],
            weight_buf.at[chunk],
            weight_sem.at[chunk],
        ).start()

    fetch(0)
    if fresh:
        count = pair_buf.shape[2]
        pltpu.make_async_copy(weight_ref.at[:, :, pl.ds(2 * ROWS, count), :], pair_buf, pair_sem.at[0]).start()
    ahead = 4 if fresh else CHUNKS
    for chunk in range(1, ahead):
        fetch(chunk)
    for chunk in range(CHUNKS):
        k, i = divmod(chunk, CHUNKS // NY)
        pltpu.make_async_copy(text_buf.at[chunk], text_buf.at[chunk], text_sem.at[chunk]).wait()
        pltpu.make_async_copy(weight_buf.at[chunk], weight_buf.at[chunk], weight_sem.at[chunk]).wait()
        if chunk + ahead < CHUNKS:
            fetch(chunk + ahead)
        part = jnp.dot(
            text_buf[chunk] * gain_ref[where_ref[1 + NY + k], :, pl.ds(i * DEEP, DEEP)],
            weight_buf[chunk].reshape(DEEP, COLS),
            preferred_element_type=jnp.float32,
        )
        acc_ref[...] = part if chunk == 0 else acc_ref[...] + part
        if fresh and chunk == 3:
            pltpu.make_async_copy(pair_buf, pair_buf, pair_sem.at[0]).wait()
            half = pair_buf.shape[2] // 2
            tall = NZ * half

            @pl.loop(0, NY)
            def _(group):
                rows = pair_buf[:, group].astype(jnp.float32)
                start = pl.multiple_of(group * tall, tall)
                for i in range(2):
                    side = rows[:, i * half : (i + 1) * half].reshape(tall, COLS)
                    side_buf[i, pl.ds(start, tall), :] = side.astype(jnp.bfloat16)

            for i, ref in enumerate((key_ref, value_ref)):
                ref[...] = jnp.dot(
                    rows_ref[...], side_buf[i], preferred_element_type=jnp.float32
                ).astype(jnp.bfloat16)

    position = where_ref[0] + lax.broadcasted_iota(jnp.int32, (TOK, KEYS), 0)
    seen = (position >= bound_ref[0:1, :]) & (position < bound_ref[1:2, :])
    anything = jnp.any(seen, axis=-1, keepdims=True)
    hidden = jnp.where(seen, 0.0, FILL)
    for head in range(COLS // HD):
        cols = pl.ds(head * HD, HD)
        queries = (acc_ref[:, cols] * scale_ref[pl.ds(TOK if fresh else 0, TOK), :]).astype(jnp.bfloat16)
        scores = lax.dot_general(
            queries, key_ref[:, cols], (((1,), (1,)), ((), ())), preferred_element_type=jnp.float32
        )
        scores = scores * (HD ** (-0.5) * LOG2E) + hidden
        highest = jnp.max(scores, axis=-1, keepdims=True)
        weights = jnp.exp2(scores - highest)
        both = jnp.concatenate([value_ref[:, cols], jnp.ones((KEYS, HD), jnp.bfloat16)], axis=1)
        mixed = jnp.dot(weights.astype(jnp.bfloat16), both, preferred_element_type=jnp.float32)
        out_ref[:, cols] = (
            mixed[:, :HD] * jnp.where(anything, 1.0 / mixed[:, HD:], 0.0)
        ).astype(jnp.bfloat16)


def attend(blocks, where, gain, scale, bounds, rows, weight):
    fresh = len(rows) == 1
    counts = tuple(len(refs) for refs in blocks)
    vmem = pl.BlockSpec(memory_space=pltpu.VMEM)
    anywhere = pl.BlockSpec(memory_space=pl.ANY)
    result = jax.ShapeDtypeStruct((TOK, COLS), jnp.bfloat16)
    pairs = weight.shape[2] - 2 * ROWS
    return pl.pallas_call(
        functools.partial(attend_kernel, counts, fresh),
        out_shape=[result] * (3 if fresh else 1),
        in_specs=[pl.BlockSpec(memory_space=pltpu.SMEM)] + [vmem] * (3 + len(rows)) + [anywhere] * (1 + sum(counts)),
        out_specs=[vmem] * (3 if fresh else 1),
        scratch_shapes=[
            pltpu.VMEM((CHUNKS, TOK, DEEP), jnp.bfloat16),
            pltpu.VMEM((CHUNKS, WIDE, 2 * ROWS, COLS), jnp.bfloat16),
            pltpu.VMEM((TOK, COLS), jnp.float32),
            pltpu.SemaphoreType.DMA((CHUNKS,)),
            pltpu.SemaphoreType.DMA((CHUNKS,)),
        ]
        + (
            [
                pltpu.VMEM((NZ, NY, pairs, COLS), jnp.bfloat16),
                pltpu.VMEM((2, VW, COLS), jnp.bfloat16),
                pltpu.SemaphoreType.DMA((1,)),
            ]
            if fresh
            else []
        ),
        compiler_params=pltpu.CompilerParams(vmem_limit_bytes=62 * 1024 * 1024),
        cost_estimate=pl.CostEstimate(
            flops=2 * TOK * COLS * (D + 2 * KEYS), bytes_accessed=18 << 20, transcendentals=TOK * KEYS * 4
        ),
    )(where, gain, scale, bounds, *rows, weight, *(ref for refs in blocks for ref in refs))


def resample_kernel(
    count_ref, image_ref, latent_ref, latent_gain_ref, context_gain_ref, query_ref, key_ref, value_ref, output_ref, out_ref
):
    latent_normed = layer_norm(
        latent_ref[...].astype(jnp.float32), latent_gain_ref[...].astype(jnp.float32)
    ).astype(jnp.bfloat16)

    def project(rows, weight_ref):
        return jnp.dot(rows, weight_ref[...], preferred_element_type=jnp.float32).astype(jnp.bfloat16)

    width = query_ref.shape[1]
    heads = width // RHD
    column = lax.broadcasted_iota(jnp.int32, (LAT, width), 1)
    masks = [(column >= h * RHD) & (column < (h + 1) * RHD) for h in range(heads)]
    latent_queries = project(latent_normed, query_ref).astype(jnp.float32)
    queries = jnp.concatenate([jnp.where(mask, latent_queries, 0.0) for mask in masks], axis=0).astype(jnp.bfloat16)
    for slot in range(image_ref.shape[0]):
        context = layer_norm(
            image_ref[slot].astype(jnp.float32), context_gain_ref[...].astype(jnp.float32)
        ).astype(jnp.bfloat16)
        joined = jnp.concatenate([context, latent_normed], axis=0)
        keys, values = project(joined, key_ref), project(joined, value_ref)
        scores = lax.dot_general(
            queries, keys, (((1,), (1,)), ((), ())), preferred_element_type=jnp.float32
        ) * RHD ** (-0.5)
        row = lax.broadcasted_iota(jnp.int32, scores.shape, 1)
        allowed = (row < count_ref[slot]) | (row >= PATCH)
        scores = jnp.where(allowed, scores, FILL)
        weights = jnp.exp(scores - jnp.max(scores, axis=-1, keepdims=True))
        probs = (weights / jnp.sum(weights, axis=-1, keepdims=True)).astype(jnp.bfloat16)
        mixed = jnp.dot(probs, values, preferred_element_type=jnp.float32)
        res_heads = sum(
            jnp.where(mask, mixed[h * LAT : (h + 1) * LAT], 0.0) for h, mask in enumerate(masks)
        ).astype(jnp.bfloat16)
        out_ref[slot] = jnp.dot(res_heads, output_ref[...], preferred_element_type=jnp.float32)


def resample(images, patch_counts, latents, latent_gain, context_gain, res_query, res_key, res_value, res_output):
    vmem = pl.BlockSpec(memory_space=pltpu.VMEM)
    return pl.pallas_call(
        resample_kernel,
        out_shape=jax.ShapeDtypeStruct((images.shape[0], LAT, VW), jnp.float32),
        in_specs=[pl.BlockSpec(memory_space=pltpu.SMEM)] + [vmem] * 8,
        out_specs=vmem,
        compiler_params=pltpu.CompilerParams(vmem_limit_bytes=40 * 1024 * 1024),
        cost_estimate=pl.CostEstimate(flops=30 << 30, bytes_accessed=8 << 20, transcendentals=1 << 18),
    )(
        patch_counts, images, latents, latent_gain[None], context_gain[None], res_query, res_key, res_value, res_output
    )


def local(
    text_rows,
    text_gain,
    query_weight,
    key_weight,
    value_weight,
    images,
    patch_counts,
    image_counts,
    image_spans,
    latents,
    latent_gain,
    context_gain,
    final_gain,
    res_query,
    res_key,
    res_value,
    res_output,
):
    y, z = lax.axis_index("y"), lax.axis_index("z")
    xh, xl, core = lax.axis_index("xh"), lax.axis_index("xl"), lax.axis_index("core")
    x = xh * 2 + xl

    def side(which):
        parts = (query_weight, key_weight, value_weight)
        return jnp.concatenate([lax.dynamic_slice_in_dim(one, which * COLS, COLS, 1) for one in parts], axis=0)

    mine, other = side(xh), flipped(side(1 - xh), ("xh",))
    low = jnp.where(xh == 0, mine, other)
    high = jnp.where(xh == 0, other, mine)
    part = key_weight.shape[0]
    pairs = jnp.concatenate([low[ROWS:], high[ROWS:]], axis=0)
    order = jnp.arange(4 * part, dtype=jnp.int32)
    block_of = jnp.asarray([0, 2, 1, 3], jnp.int32)[order // part] * part + order % part
    pairs = jnp.dot(
        (block_of[:, None] == order[None, :]).astype(jnp.bfloat16), pairs, preferred_element_type=jnp.float32
    ).astype(jnp.bfloat16)
    weight = lax.all_gather(jnp.concatenate([low[:ROWS], high[:ROWS], pairs], axis=0), ("z", "y"), axis=0)
    weight = weight.reshape(NZ, NY, -1, COLS)

    source = text_rows.astype(jnp.float32)
    power = jnp.sum(source * source, axis=-1)
    live_slot = jnp.arange(2, dtype=jnp.int32) < image_counts[0]
    span_bounds = jnp.where(live_slot[None, :], image_spans, 0)
    mix = resample(
        images, patch_counts, latents, latent_gain, context_gain, res_query, res_key, res_value, res_output
    ).reshape(2, 2, LAT // 2, VW)
    small = jnp.concatenate(
        [
            power,
            text_gain.astype(jnp.float32),
            span_bounds.reshape(4).astype(jnp.float32),
            next_pair(after(span_bounds.reshape(4).astype(jnp.float32), mix)),
            jnp.zeros((4 * VW - TOK - D // NY - 8,), jnp.float32),
        ]
    ).reshape(1, 4, VW)
    text_out = after(text_rows, other)
    cut = TOK // 2
    halves = (text_out[:cut], text_out[cut:])
    near_bottom, cross_top = flipped(halves[1], ("xl",)), flipped(halves[0], ("xh", "xl"))
    cross_top, near_bottom, mix = lax.optimization_barrier((cross_top, near_bottom, mix))
    sent = jnp.concatenate(
        [lax.dynamic_index_in_dim(mix, 1 - core, 1, keepdims=False).reshape(LAT, VW), small[0]], axis=0
    )
    got = flipped(sent, ("core",))
    first = lax.dynamic_index_in_dim(mix, core, 1, keepdims=False) + got[:LAT].reshape(2, LAT // 2, VW)
    small = jnp.stack([small[0], got[LAT:]])
    sent = jnp.concatenate([lax.dynamic_index_in_dim(first, 1 - xl, 0, keepdims=False), small.reshape(8, VW)], axis=0)
    got = flipped(sent, ("xl",))
    small = small.reshape(2, 4 * VW)
    short = jnp.concatenate([jnp.sum(small[:, :TOK], axis=0), small[0, TOK + D // NY :][:128]])
    cross_top, near_bottom, *halves, got = lax.optimization_barrier((cross_top, near_bottom, *halves, got))
    near_text = [flipped(halves[0], ("xl",)), near_bottom]
    cross_text = [cross_top, flipped(halves[1], ("xh", "xl"))]
    far_text = [flipped(cross_top, ("xl",)), flipped(near_bottom, ("xh", "xl"))]
    total = lax.dynamic_index_in_dim(first, xl, 0, keepdims=False) + got[: LAT // 2]
    small = jnp.concatenate([small, got[LAT // 2 :].reshape(2, 4 * VW)], axis=0)

    base = lax.dynamic_slice_in_dim(latents, core * (LAT // 2), LAT // 2, 0).astype(jnp.float32)
    piece = layer_norm(base + total, final_gain.astype(jnp.float32)).astype(jnp.bfloat16)
    both = jnp.stack([next_pair(piece), piece])
    near_text[0], cross_text[1], *far_text, both = lax.optimization_barrier(
        (near_text[0], cross_text[1], *far_text, both)
    )
    both, short_cross, short_far = lax.optimization_barrier(
        (jnp.stack([both, flipped(both, ("xl",))]), flipped(short, ("xh", "xl")), flipped(short, ("xh",)))
    )

    swap = lambda rows: [flipped(one, ("core",)) for one in rows]
    our_blocks = [[text_rows], swap([text_rows]), near_text, swap(near_text)]
    their_blocks = [cross_text, swap(cross_text), far_text, swap(far_text)]
    power = jnp.concatenate([jnp.sum(small[:, :TOK], axis=0), short_cross[:TOK] + short_far[:TOK]])
    scale = lax.rsqrt(power / D + EPS_TEXT).reshape(2 * TOK, 1)
    gain = small[:, TOK : TOK + D // NY].astype(jnp.bfloat16).reshape(NY, 1, D // NY)
    spans = [one[TOK : TOK + 8].reshape(2, 2, 2) for one in (short, short_far)]
    spans = jnp.where(xh == 0, jnp.concatenate(spans, axis=2), jnp.concatenate(spans[::-1], axis=2))
    near = jnp.stack([spans[1], spans[0]], axis=1)
    near = jnp.take(near, x ^ jnp.arange(NX), axis=2).transpose(0, 2, 1).reshape(2, 8).astype(jnp.int32)
    bounds = jnp.tile(jnp.repeat(near, LAT // 2, axis=1), (1, 2))

    both = jnp.stack([both, flipped(both, ("xh",))])
    around = jnp.stack([both[0, 0], both[0, 1], both[1, 0], both[1, 1]])
    resampled = jnp.concatenate([around, turned(around, "core", 1, 2)], axis=0).reshape(KEYS, VW)

    def half(blocks, which, others, rows):
        places = [2 * p + q for p, q in ((others, core), (others, 1 - core), (1 - others, core), (1 - others, 1 - core))]
        turns = [place ^ (2 * xl + core) for place in places]
        where = jnp.stack([(y * NZ + z) * (2 * TOK) + which * TOK, *places, *turns]).astype(jnp.int32)
        return attend(blocks, where, gain, scale, bounds, rows, weight)

    theirs, keys, values = half(their_blocks, 1 - xh, 1 - xl, (resampled,))
    received = flipped(theirs, ("xh",))
    (ours,) = half(our_blocks, xh, xl, (keys, values))
    return jnp.where(
        xh == 0,
        jnp.concatenate([ours, received], axis=1),
        jnp.concatenate([received, ours], axis=1),
    )


def solution(mesh):
    fine = Mesh(mesh.devices.reshape(NY, NZ, 2, 2, 2), ("y", "z", "xh", "xl", "core"))
    seq = ("y", "z", "xh")
    head = ("xl", "core")
    return jax.shard_map(
        local,
        mesh=fine,
        in_specs=(
            P(seq, head),
            P(head),
            P(seq, head),
            P(seq, head),
            P(seq, head),
            P(seq, None, None),
            P(seq),
            P(seq),
            P(None, seq),
            P(),
            P(),
            P(),
            P(),
            P(None, head),
            P(None, head),
            P(None, head),
            P(head, None),
        ),
        out_specs=P(seq, head),
        check_vma=False,
    )
```
